32 devices in a mesh: groups: 2 (over x), stream: 16 (over z, y, core).
Axes of the slice: x: 2, y: 2, z: 4, core: 2. Of those that a mesh axis runs over, the one named last changes fastest.
Arguments:
- hidden_units: bfloat16 [64, 3584], P('groups', 'stream'), parts along dimension 0, may hold values from -6 to 6
- residual: bfloat16 [64, 8192], P(('groups', 'stream')), parts along dimension 0, may hold values from -6 to 6
- down_weight: bfloat16 [3584, 8192], P('stream'), may hold values from -0.09375 to 0.09375
- final_gain: bfloat16 [8192], replicated, may hold values from 0.5 to 1.5
- head_weight: bfloat16 [8192, 8192], P('stream'), may hold values from -0.19824219 to 0.19824219
- targets: int32 [64], P('groups'), parts along dimension 0, may hold values from 0 to 8191
- segments: int32 [64], P(('groups', 'stream')), parts along dimension 0, may hold values from 1 to 4, as said below
- train_loss: float32 [64], P(('groups', 'stream')), parts along dimension 0, may hold values from 12 to 20
Outputs:
- hidden_states: bfloat16 [64, 8192], P(('groups', 'stream')), parts along dimension 0
- loss_weight: float32 [64], P(('groups', 'stream')), parts along dimension 0
The draws below stay inside these ranges and needn't reach their ends.
There are 2 independent parts, one for each index of `groups`. The reference program is written for one: setup_inputs(seed, part) draws one part's arguments, and reference() takes and returns one part's arrays. A program takes and returns all parts, laid end to end along the dimension named above; an argument that names none is the same for every part. Nothing has to cross between parts.
Inputs may be any that keep to these rules, and one draw needn't show every extreme that they name: `segments`: document numbers start at 1 and rise by one at each new document; the first document holds exactly the first 16 tokens; every later aligned block of 16 tokens begins a document at its first token and begins exactly two more inside it, so each document holds 1 to 16 consecutive tokens.
All inputs are finite; a program needn't handle non-finite values.
Results may differ from the reference program's by a relative error of at most 0.0083.
Values may be sent and summed in bfloat16 or wider, within the bound.
No kernel may reach another device: no remote copies, remote signals or barrier semaphores. Data moves between devices by JAX's collectives and lax.ppermute only.
A program may use at most 128 MiB of HBM per device.

```python
import jax
import jax.numpy as jnp
from jax import lax

D = 8192
TOKENS = 32
FF = 3584
VOCAB = 8192


def draw_segments(key, part):
    key = jax.random.fold_in(key, 7)
    key_low, key_high = jax.random.split(key)
    block_count = TOKENS // 16
    low_offset = jax.random.randint(key_low, (block_count,), 1, 8, dtype=jnp.int32)
    high_offset = jax.random.randint(key_high, (block_count,), 8, 15, dtype=jnp.int32)
    places = jnp.arange(TOKENS, dtype=jnp.int32)
    offsets = places % 16
    blocks = places // 16
    starts = (blocks > 0) & ((offsets == 0) | (offsets == low_offset[blocks]) | (offsets == high_offset[blocks]))
    return (1 + jnp.cumsum(starts.astype(jnp.int32))).astype(jnp.int32)


def place_ends(result, key, least, top_value):
    spot = [jax.random.randint(jax.random.fold_in(key, axis), (), 0, length) for axis, length in enumerate(result.shape)]
    longest = result.shape.index(max(result.shape))
    neighbour = spot[:longest] + [(spot[longest] + 1) % result.shape[longest]] + spot[longest + 1:]
    return result.at[tuple(spot)].set(least).at[tuple(neighbour)].set(top_value)


def with_spikes(array, key, source, target, shards_of, factor):
    def block_of(axis_at):
        return (jnp.arange(array.shape[axis_at]) // (array.shape[axis_at] // shards_of)).reshape((-1,) + (1,) * (array.ndim - 1 - axis_at))

    near = jax.random.permutation(key, shards_of)[block_of(target)]
    other_side = (block_of(target) + shards_of // 2) % shards_of
    return jnp.where((block_of(source) == near) | (block_of(source) == other_side), factor * array, array)


def shard_levels(key, dims, pieces, smallest, high):
    gain, own = 1.0, jax.random.fold_in(key, 6)
    for axis_at, parts in pieces:
        heights = jnp.exp(jax.random.uniform(jax.random.fold_in(own, axis_at), (parts,), jnp.float32, smallest / len(pieces), high / len(pieces)))
        gain = gain * jnp.repeat(heights, dims[axis_at] // parts).reshape([-1 if axis == axis_at else 1 for axis in range(len(dims))])
    return gain


def gaussian(key, dims, width, reach, pieces=(), kind=jnp.bfloat16):
    array = jax.random.normal(key, dims, jnp.float32) * width
    if len(pieces) > 0:
        array = shard_levels(key, dims, pieces, -0.22, 0.18) * array
    return jnp.clip(array, min=-reach, max=reach).astype(kind)


def bell_draw_with(rng, extent, width, reach, pieces, heavy, held_as=jnp.bfloat16):
    drawn = width * jax.random.normal(rng, extent, jnp.float32)
    if pieces:
        drawn = drawn * shard_levels(rng, extent, pieces, -0.22, 0.18)
    return jnp.clip(with_spikes(drawn, jax.random.fold_in(rng, 3), *heavy), -reach, reach).astype(held_as)


def setup_inputs(seed: int = 0, part: int = 0) -> dict:
    seeds = jax.random.split(jax.random.key(seed), 9)
    own_keys = jax.random.split(jax.random.fold_in(seeds[8], part), 9)
    hidden_units = bell_draw_with(own_keys[0], (TOKENS, FF), 1.0, 6.0, ((1, 16),), (1, 0, 16, 2.0))
    residual = gaussian(own_keys[1], (TOKENS, D), 1.0, 6.0, ((0, 16),))
    down_weight = gaussian(seeds[2], (FF, D), FF ** -0.5, 0.09375, ((0, 16),))
    final_gain = jnp.clip(1.0 + 0.1 * jax.random.normal(seeds[3], (D,), jnp.float32), 0.5, 1.5).astype(jnp.bfloat16)
    head_weight = gaussian(seeds[4], (VOCAB, D), (3 * D ** -0.5), 0.19824219, ((0, 16),))
    targets = place_ends(jax.random.randint(own_keys[5], (TOKENS,), 0, VOCAB), jax.random.fold_in(own_keys[5], 1), 0, VOCAB - 1).astype(jnp.int32)
    segments = draw_segments(jax.random.fold_in(jax.random.fold_in(seeds[8], part), 71), part)
    train_loss = jnp.clip(12.0 + 8.0 * jax.random.uniform(own_keys[7], (TOKENS,), jnp.float32) ** shard_levels(own_keys[7], (TOKENS,), ((0, 16),), -0.2, 0.2), 12.0, 20.0)
    return dict(hidden_units=hidden_units, residual=residual, down_weight=down_weight, final_gain=final_gain, head_weight=head_weight, targets=targets, segments=segments, train_loss=train_loss)


def normalize(states, final_gain):
    values = states.astype(jnp.float32)
    mean_sq = lax.optimization_barrier(jnp.mean(values * values, axis=-1, keepdims=True))
    return (values * jax.lax.rsqrt(mean_sq + 1e-05) * final_gain.astype(jnp.float32)).astype(jnp.bfloat16)

def reference(hidden_units, residual, down_weight, final_gain, head_weight, targets, segments, train_loss):
    ffn_out = jnp.dot(hidden_units, down_weight, preferred_element_type=jnp.float32)
    hidden_states = (residual.astype(jnp.float32) + ffn_out).astype(jnp.bfloat16)
    normed = normalize(hidden_states, final_gain)
    logits = jnp.dot(normed, head_weight.T, preferred_element_type=jnp.float32)
    sum_exp = lax.optimization_barrier(jnp.sum(jnp.exp(logits), axis=1))
    target_logit = jnp.take_along_axis(logits, targets[:, None].astype(jnp.int32), axis=1)[:, 0]
    ref_loss = jnp.log(sum_exp) - target_logit
    next_ids = jnp.concatenate([segments[1:], jnp.full((1,), -1, jnp.int32)])
    same_doc = (next_ids == segments).astype(jnp.float32)
    loss_weight = same_doc * jax.nn.sigmoid(train_loss - ref_loss)
    return (hidden_states, loss_weight)
```

```python
import jax
import jax.numpy as jnp
import numpy as np
from jax import lax
from jax.sharding import PartitionSpec as P

AXIS = "stream"
F32 = jnp.float32
BF16 = jnp.bfloat16


def levels_of(devices):
    levels, stride = [(1, 2)], 2
    while stride < devices:
        size = 4 if (devices // stride) % 4 == 0 else 2
        levels.append((stride, size))
        stride *= size
    assert stride == devices
    return levels


def offsets_of(levels):
    offsets = np.zeros((1,), np.int32)
    for stride, size in levels:
        offsets = (offsets[:, None] + stride * np.arange(size, dtype=np.int32)[None, :]).reshape(-1)
    return offsets


def swapped(block, distance):
    return lax.ppermute(block, AXIS, [(i, i ^ distance) for i in range(lax.axis_size(AXIS))])


def fold(block, level):
    stride, size = level
    parts = block.reshape((size, -1) + block.shape[1:])
    came = [swapped(parts[k], stride * k) for k in range(size - 1, 0, -1)]
    return sum(came, parts[0])


def exchange(block, level):
    stride, size = level
    parts = block.reshape((size, -1) + block.shape[1:])
    came = {k: swapped(parts, stride * k) for k in range(size - 1, 0, -1)}
    out = []
    for place in range(size):
        terms = [(k, came[k][place ^ k]) for k in range(1, size)] + [(0, parts[place])]
        out.append(sum((t for _, t in terms[1:]), terms[0][1]))
    return jnp.stack(out).reshape(block.shape)


def spread(block, level):
    stride, size = level
    came = {k: swapped(block, stride * k) for k in range(size - 1, 0, -1)}
    return jnp.concatenate([block] + [came[k] for k in range(1, size)], axis=0)


def on_device(
    hidden_units, residual, down_weight, final_gain, head_weight, targets, segments, train_loss
):
    own = residual.shape[0]
    tokens = hidden_units.shape[0]
    vocab_rows = head_weight.shape[0]
    devices = lax.axis_size(AXIS)
    device_index = lax.axis_index(AXIS)
    levels = levels_of(devices)
    offsets = offsets_of(levels)

    holder = device_index ^ jnp.asarray(offsets)
    places = (holder[:, None] * own + jnp.arange(own, dtype=jnp.int32)[None, :]).reshape(-1)
    chosen = places[:, None] == lax.broadcasted_iota(jnp.int32, (tokens, tokens), 1)
    hidden = jnp.dot(chosen.astype(BF16), hidden_units, preferred_element_type=F32).astype(BF16)
    row_targets = jnp.sum(jnp.where(chosen, targets[None, :], 0), axis=1)

    part = jnp.dot(hidden, down_weight, preferred_element_type=F32)
    for level in levels[:-1]:
        part = fold(part, level)
    part = jnp.concatenate([part[:own] + residual.astype(F32), part[own:]], axis=0)
    states = exchange(part, levels[-1]).astype(BF16)
    hidden_states = states[:own]
    values = states.astype(F32)
    mean_sq = jnp.mean(values * values, axis=-1, keepdims=True)
    normed = (values * lax.rsqrt(mean_sq + 1e-05) * final_gain.astype(F32)).astype(BF16)
    for level in levels[-2::-1]:
        normed = spread(normed, level)

    logits = jnp.einsum("td,vd->tv", normed, head_weight, preferred_element_type=F32)
    sum_exp = jnp.sum(jnp.exp(logits), axis=1)
    vocab_ids = device_index * vocab_rows + lax.broadcasted_iota(jnp.int32, logits.shape, 1)
    target_logit = jnp.sum(jnp.where(row_targets[:, None] == vocab_ids, logits, 0.0), axis=1)
    before_own = places == device_index * own - 1
    next_first = jnp.where(before_own, segments[0].astype(F32), 0.0)
    message = jnp.stack([sum_exp, target_logit, next_first], axis=1)
    for level in levels:
        message = fold(message, level)

    ref_loss = jnp.log(message[:, 0]) - message[:, 1]
    next_ids = jnp.concatenate([segments[1:], message[own - 1 :, 2].astype(jnp.int32)])
    positions = device_index * own + jnp.arange(own, dtype=jnp.int32)
    same_doc = jnp.where((positions + 1 < tokens) & (next_ids == segments), 1.0, 0.0)
    loss_weight = same_doc.astype(F32) * jax.nn.sigmoid(train_loss - ref_loss)
    return (hidden_states, loss_weight)


def solution(mesh):
    placed = (
        P("groups", "stream"),
        P(("groups", "stream"), None),
        P("stream", None),
        P(),
        P("stream", None),
        P("groups"),
        P(("groups", "stream")),
        P(("groups", "stream")),
    )
    return jax.shard_map(
        on_device,
        mesh=mesh,
        in_specs=placed,
        out_specs=(P(("groups", "stream"), None), P(("groups", "stream"))),
        check_vma=False,
    )
```

```python
import functools

import jax
import jax.numpy as jnp
from jax import lax
from jax.experimental import pallas as pl
from jax.experimental.pallas import tpu as pltpu
from jax.sharding import PartitionSpec as P

AXIS = "stream"
F32 = jnp.float32
BF16 = jnp.bfloat16
I32 = jnp.int32
WHOLE = pl.BlockSpec(memory_space=pltpu.VMEM)


def levels_of(devices):
    levels, stride = [(1, 2)], 2
    while stride < devices:
        size = 4 if (devices // stride) % 4 == 0 else 2
        levels.append((stride, size))
        stride *= size
    assert stride == devices
    return levels


def log2(number):
    assert number & (number - 1) == 0
    return number.bit_length() - 1


def swapped(block, distance):
    return lax.ppermute(block, AXIS, [(i, i ^ distance) for i in range(lax.axis_size(AXIS))])


def bytes_of(*arrays):
    return sum(a.size * a.dtype.itemsize for a in arrays)


def call(body, outs, *operands, extra=0, scratch=(), specs=None):
    shapes = [jax.ShapeDtypeStruct(shape, kind) for shape, kind in outs]
    return pl.pallas_call(
        body,
        out_shape=shapes,
        in_specs=specs or [WHOLE] * len(operands),
        out_specs=[WHOLE] * len(shapes),
        scratch_shapes=scratch,
        compiler_params=pltpu.CompilerParams(
            vmem_limit_bytes=bytes_of(*operands, *shapes) * 5 // 4 + extra + (2 << 20)
        ),
    )(*operands)


def token_at(place, levels, own):
    holder, inner = place >> log2(own), 1
    offset = jnp.zeros_like(place)
    for stride, size in reversed(levels):
        offset += ((holder >> log2(inner)) & (size - 1)) * stride
        inner *= size
    return (lax.axis_index(AXIS) ^ offset) * own + (place & (own - 1))


def ffn_kernel(levels, own, vocab_rows, *refs):
    sources, (keep_ref, send_ref, facts_ref, residual_ref, gain_ref, segments_ref, train_ref) = refs[:7], refs[7:14]
    hidden_ref, targets_ref, weights, arrived, loaded = refs[14:]
    hidden_hbm, targets_hbm, down_hbm = sources[:3]
    tokens = hidden_ref.shape[0]
    columns = down_hbm.shape[1] // CHUNKS
    copies = [
        pltpu.make_async_copy(
            down_hbm.at[:, pl.ds(c * columns, columns)], weights.at[c], arrived.at[c]
        )
        for c in range(CHUNKS)
    ]
    pairs = ((hidden_hbm, hidden_ref), (targets_hbm, targets_ref)) + tuple(
        zip(sources[3:], (residual_ref, gain_ref, segments_ref, train_ref))
    )
    small = [pltpu.make_async_copy(*pair, loaded.at[i]) for i, pair in enumerate(pairs)]
    small[0].start()
    for copy in copies + small[1:]:
        copy.start()
    square = (tokens, tokens)
    at_row = token_at(lax.broadcasted_iota(I32, square, 0), levels, own)
    chosen = at_row == lax.broadcasted_iota(I32, square, 1)
    small[0].wait()
    rows = jnp.dot(
        chosen.astype(F32).astype(BF16), hidden_ref[...], preferred_element_type=F32
    ).astype(BF16)
    for c in range(CHUNKS):
        copies[c].wait()
        part = jnp.dot(rows, weights[c], preferred_element_type=F32)
        keep_ref[:, c * columns : (c + 1) * columns] = part[: tokens // 2]
        send_ref[:, c * columns : (c + 1) * columns] = part[tokens // 2 :]
    for copy in small[1:]:
        copy.wait()
    wanted = jnp.sum(jnp.where(chosen, targets_ref[...], 0), axis=1, keepdims=True)
    diagonal = lax.broadcasted_iota(I32, square, 0) == lax.broadcasted_iota(I32, square, 1)
    wanted = jnp.sum(jnp.where(diagonal, wanted, 0), axis=0, keepdims=True)
    me = lax.axis_index(AXIS)
    facts_ref[0:1, :] = wanted - me * vocab_rows
    at_lane = token_at(lax.broadcasted_iota(I32, (1, tokens), 1), levels, own)
    following = jnp.zeros((1, tokens), I32)
    for j in range(own):
        following = jnp.where(at_lane + 1 == me * own + j, segments_ref[0:1, j : j + 1], following)
    facts_ref[1:2, :] = following


CHUNKS = 4


def add_kernel(came_count, keep_ref, *refs):
    total = keep_ref[...]
    for ref in refs[:came_count]:
        total += ref[...]
    outs = refs[came_count:]
    rows = total.shape[0] // len(outs)
    for k, out in enumerate(outs):
        out[...] = total[k * rows : (k + 1) * rows]


def add_residual_kernel(came_count, keep_ref, residual_ref, *refs):
    total = keep_ref[...]
    for ref in refs[:came_count]:
        total += ref[...]
    out = refs[came_count]
    own = residual_ref.shape[0]
    out[:own, :] = total[:own] + residual_ref[...].astype(F32)
    out[own:, :] = total[own:]


def norm_kernel(size, own, head_ref, gain_ref, mine_ref, *refs):
    del head_ref
    came, (states_ref, normed_ref) = refs[: size - 1], refs[size - 1 :]
    for place in range(size):
        total = mine_ref[place * own : (place + 1) * own, :]
        for k in range(1, size):
            total = total + came[k - 1][(place ^ k) * own : ((place ^ k) + 1) * own, :]
        states = total.astype(BF16)
        if place == 0:
            states_ref[...] = states
        values = states.astype(F32)
        scale = lax.rsqrt(jnp.mean(values * values, axis=1, keepdims=True) + 1e-05)
        for c in range(gain_ref.shape[0]):
            at = slice(c * 128, (c + 1) * 128)
            normed = values[:, at] * scale * gain_ref[c : c + 1, :].astype(F32)
            normed_ref[place * own : (place + 1) * own, at] = normed.astype(BF16)


def copy_kernel(source, out):
    out[...] = source[...]


def load_kernel(source, out, arrived):
    copy = pltpu.make_async_copy(source, out, arrived)
    copy.start()
    copy.wait()


def join_kernel(*refs):
    blocks, out = refs[1:-1], refs[-1]
    out[...] = jnp.concatenate([b[...].astype(F32) for b in blocks], axis=0).astype(BF16)


def loss_kernel(facts_ref, head_ref, near_ref, far_ref, keep_ref, send_ref):
    rows = jnp.concatenate([near_ref[...], far_ref[...]], axis=0)
    logits = lax.dot_general(
        head_ref[...], rows, (((1,), (1,)), ((), ())), preferred_element_type=F32
    )
    ids = lax.broadcasted_iota(I32, logits.shape, 0)
    half = rows.shape[0] // 2
    total = jnp.sum(jnp.exp(logits), axis=0, keepdims=True)
    picked = jnp.sum(jnp.where(ids == facts_ref[0:1, :], logits, 0.0), axis=0, keepdims=True)
    for row, values in enumerate((total, picked, facts_ref[1:2, :].astype(F32))):
        keep_ref[row : row + 1, :] = values[:, :half]
        send_ref[row : row + 1, :] = values[:, half:]


def add_lanes_kernel(came_count, keep_ref, *refs):
    total = keep_ref[...]
    for ref in refs[:came_count]:
        total += ref[...]
    outs = refs[came_count:]
    lanes = total.shape[1] // len(outs)
    for k, out in enumerate(outs):
        out[...] = total[:, k * lanes : (k + 1) * lanes]


def weight_kernel(tokens, came_count, segments_ref, train_ref, keep_ref, *refs):
    total = keep_ref[...]
    for ref in refs[:came_count]:
        total += ref[...]
    out = refs[came_count]
    own = out.shape[1]
    ref_loss = jnp.log(total[0:1]) - total[1:2]
    places = lax.axis_index(AXIS) * own + lax.broadcasted_iota(I32, (1, own), 1)
    same = (places + 1 < tokens) & (total[2:3].astype(I32) == segments_ref[...])
    out[...] = jnp.where(same, jax.nn.sigmoid(train_ref[...] - ref_loss), 0.0)


def on_device(
    hidden_units, residual, down_weight, final_gain, head_weight, targets, segments, train_loss
):
    own, width = residual.shape
    tokens, depth = hidden_units.shape
    levels = levels_of(lax.axis_size(AXIS))
    segments, train_loss = segments[None, :], train_loss[None, :]

    half = (tokens // 2, width)
    gain = final_gain.reshape(-1, 128)
    sources = [hidden_units, targets[None, :], down_weight, residual, gain, segments, train_loss]
    keep, send, facts, residual, gain, segments, train_loss = call(
        functools.partial(ffn_kernel, levels, own, head_weight.shape[0]),
        [(half, F32), (half, F32), ((2, tokens), I32)] + [(a.shape, a.dtype) for a in sources[3:]],
        *[pltpu.with_memory_space_constraint(a, pltpu.HBM) for a in sources],
        extra=bytes_of(down_weight),
        scratch=(
            pltpu.VMEM(hidden_units.shape, BF16),
            pltpu.VMEM((1, tokens), I32),
            pltpu.VMEM((CHUNKS, depth, width // CHUNKS), BF16),
            pltpu.SemaphoreType.DMA((CHUNKS,)),
            pltpu.SemaphoreType.DMA((6,)),
        ),
        specs=[pl.BlockSpec(memory_space=pltpu.HBM)] * 7,
    )
    came, rows = [swapped(send, 1)], tokens // 2
    for stride, size in levels[1:-1]:
        rows //= size
        keep, *parts = call(
            functools.partial(add_kernel, len(came)), [((rows, width), F32)] * size, keep, *came
        )
        came = [swapped(parts[k - 1], stride * k) for k in range(1, size)]
    stride, size = levels[-1]
    (mine,) = call(
        functools.partial(add_residual_kernel, len(came)), [((rows, width), F32)], keep, residual, *came
    )
    came = [swapped(mine, stride * k) for k in range(1, size)]
    (head,) = call(
        load_kernel,
        [(head_weight.shape, BF16)],
        pltpu.with_memory_space_constraint(head_weight, pltpu.HBM),
        scratch=(pltpu.SemaphoreType.DMA,),
        specs=[pl.BlockSpec(memory_space=pltpu.HBM)],
    )
    states, block = call(
        functools.partial(norm_kernel, size, own),
        [((own, width), BF16), ((rows, width), BF16)],
        head,
        gain,
        mine,
        *came,
        specs=[pl.BlockSpec(memory_space=pl.ANY)] + [WHOLE] * (size + 1),
    )
    (hidden_states,) = call(copy_kernel, [(states.shape, BF16)], states)
    for stride, size in levels[-2:0:-1]:
        came = [swapped(block, stride * k) for k in range(1, size)]
        (block,) = call(
            join_kernel,
            [((rows * size, width), BF16)],
            pltpu.with_memory_space_constraint(hidden_states, pltpu.HBM),
            block,
            *came,
            extra=bytes_of(block) * 8,
            specs=[pl.BlockSpec(memory_space=pltpu.HBM)] + [WHOLE] * size,
        )
        rows *= size
    far = swapped(block, 1)

    keep, send = call(
        loss_kernel,
        [((3, tokens // 2), F32)] * 2,
        facts,
        head,
        block,
        far,
        extra=2 * bytes_of(block),
    )
    came, lanes = [swapped(send, 1)], tokens // 2
    for stride, size in levels[1:]:
        lanes //= size
        keep, *parts = call(
            functools.partial(add_lanes_kernel, len(came)), [((3, lanes), F32)] * size, keep, *came
        )
        came = [swapped(parts[k - 1], stride * k) for k in range(1, size)]
    (loss_weight,) = call(
        functools.partial(weight_kernel, tokens, len(came)), [((1, own), F32)], segments, train_loss, keep, *came
    )
    return (hidden_states, loss_weight.reshape(own))


def solution(mesh):
    placed = (
        P("groups", "stream"),
        P(("groups", "stream"), None),
        P("stream", None),
        P(),
        P("stream", None),
        P("groups"),
        P(("groups", "stream")),
        P(("groups", "stream")),
    )
    return jax.shard_map(
        on_device,
        mesh=mesh,
        in_specs=placed,
        out_specs=(P(("groups", "stream"), None), P(("groups", "stream"))),
        check_vma=False,
    )
```

```python
import functools

import jax
import jax.numpy as jnp
from jax import lax
from jax.experimental import pallas as pl
from jax.experimental.pallas import tpu as pltpu
from jax.sharding import PartitionSpec as P

AXIS = "stream"
F32 = jnp.float32
BF16 = jnp.bfloat16
F16 = jnp.float16
I32 = jnp.int32
WHOLE = pl.BlockSpec(memory_space=pltpu.VMEM)
IN_HBM = pl.BlockSpec(memory_space=pltpu.HBM)
ANYWHERE = pl.BlockSpec(memory_space=pl.ANY)
CHUNKS = 4


def levels_of(devices, crossed):
    levels, stride = [(0, 1)], 2
    while stride < devices:
        if (devices // stride) % 4 == 0:
            levels.append((0, stride | crossed, 2 * stride | crossed, 3 * stride))
        else:
            levels.append((0, stride | crossed))
        stride *= len(levels[-1])
    assert stride == devices
    return levels


def log2(number):
    assert number & (number - 1) == 0
    return number.bit_length() - 1


def swapped(block, distance):
    return lax.ppermute(block, AXIS, [(i, i ^ distance) for i in range(lax.axis_size(AXIS))])


def bytes_of(*arrays):
    return sum(a.size * a.dtype.itemsize for a in arrays)


def call(body, outs, *operands, extra=0, scratch=(), specs=None):
    shapes = [jax.ShapeDtypeStruct(shape, kind) for shape, kind in outs]
    return pl.pallas_call(
        body,
        out_shape=shapes,
        in_specs=specs or [WHOLE] * len(operands),
        out_specs=[WHOLE] * len(shapes),
        scratch_shapes=scratch,
        compiler_params=pltpu.CompilerParams(
            vmem_limit_bytes=bytes_of(*operands, *shapes) * 5 // 4 + extra + (2 << 20)
        ),
    )(*operands)


def distance_at(holder, levels):
    distance, inner = jnp.zeros_like(holder), 0
    for level in reversed(levels):
        digit = holder >> inner
        for bit in range(log2(len(level))):
            distance ^= ((digit >> bit) & 1) * level[1 << bit]
        inner += log2(len(level))
    return distance


def token_at(place, levels, own):
    distance = distance_at(place >> log2(own), levels)
    return (lax.axis_index(AXIS) ^ distance) * own + (place & (own - 1))


def ffn_kernel(levels, gather_levels, own, vocab_rows, *refs):
    sources, (keep_ref, send_ref, facts_ref, residual_ref, gain_ref, segments_ref, train_ref) = refs[:7], refs[7:14]
    hidden_ref, targets_ref, weights, arrived, loaded = refs[14:]
    hidden_hbm, targets_hbm, down_hbm = sources[:3]
    tokens = hidden_ref.shape[0]
    columns = down_hbm.shape[1] // CHUNKS
    copies = [
        pltpu.make_async_copy(
            down_hbm.at[:, pl.ds(c * columns, columns)], weights.at[c], arrived.at[c]
        )
        for c in range(CHUNKS)
    ]
    pairs = ((hidden_hbm, hidden_ref), (targets_hbm, targets_ref)) + tuple(
        zip(sources[3:], (residual_ref, gain_ref, segments_ref, train_ref))
    )
    small = [pltpu.make_async_copy(*pair, loaded.at[i]) for i, pair in enumerate(pairs)]
    small[0].start()
    for copy in copies + small[1:]:
        copy.start()
    square = (tokens, tokens)
    sublane, lane = (lax.broadcasted_iota(I32, square, d) for d in (0, 1))
    chosen = token_at(sublane, levels, own) == lane
    small[0].wait()
    rows = jnp.dot(
        chosen.astype(F32).astype(BF16), hidden_ref[...], preferred_element_type=F32
    ).astype(BF16)
    for c in range(CHUNKS):
        copies[c].wait()
        part = jnp.dot(rows, weights[c], preferred_element_type=F32)
        keep_ref[:, c * columns : (c + 1) * columns] = part[: tokens // 2]
        send_ref[:, c * columns : (c + 1) * columns] = part[tokens // 2 :]
    for copy in small[1:]:
        copy.wait()
    chosen = token_at(sublane, gather_levels, own) == lane
    wanted = jnp.sum(jnp.where(chosen, targets_ref[...], 0), axis=1, keepdims=True)
    wanted = jnp.sum(jnp.where(sublane == lane, wanted, 0), axis=0, keepdims=True)
    me = lax.axis_index(AXIS)
    facts_ref[0:1, :] = wanted - me * vocab_rows
    at_lane = token_at(lax.broadcasted_iota(I32, (1, tokens), 1), gather_levels, own)
    following = jnp.zeros((1, tokens), I32)
    for j in range(own):
        following = jnp.where(at_lane + 1 == me * own + j, segments_ref[0:1, j : j + 1], following)
    facts_ref[1:2, :] = following


def norm_kernel(own, total_ref, gain_ref, states_ref, normed_ref):
    states = total_ref[...].astype(BF16)
    states_ref[...] = states[:own]
    values = states.astype(F32)
    scale = lax.rsqrt(jnp.mean(values * values, axis=1, keepdims=True) + 1e-05)
    for c in range(gain_ref.shape[0]):
        at = slice(c * 128, (c + 1) * 128)
        normed_ref[:, at] = (values[:, at] * scale * gain_ref[c : c + 1, :].astype(F32)).astype(BF16)


def copy_kernel(source, out):
    out[...] = source[...]


def load_kernel(first, source, after, out, arrived):
    copy = pltpu.make_async_copy(source.at[pl.ds(first, out.shape[0])], out, arrived)
    copy.start()
    copy.wait()


def join_kernel(*refs):
    blocks, out = refs[1:-1], refs[-1]
    out[...] = jnp.concatenate([b[...].astype(F32) for b in blocks], axis=0).astype(BF16)


def loss_kernel(own, gather_levels, sum_levels, head_count, facts_ref, *refs):
    heads, (near_ref, far_ref, keep_ref, send_ref) = refs[:head_count], refs[head_count:]
    rows = jnp.concatenate([near_ref[...], far_ref[...]], axis=0)
    half, first, total, picked = rows.shape[0] // 2, 0, 0.0, 0.0
    for head_ref in heads:
        logits = lax.dot_general(
            head_ref[...], rows, (((1,), (1,)), ((), ())), preferred_element_type=F32
        )
        ids = lax.broadcasted_iota(I32, logits.shape, 0) + first
        total += jnp.sum(jnp.exp(logits), axis=0, keepdims=True)
        picked += jnp.sum(jnp.where(ids == facts_ref[0:1, :], logits, 0.0), axis=0, keepdims=True)
        first += head_ref.shape[0]
    holder = lax.broadcasted_iota(I32, (1, half), 1) >> log2(own)
    other = ((distance_at(holder, gather_levels[1:]) ^ distance_at(holder, sum_levels[1:])) & 1) == 1
    for row, values in enumerate((total, picked, facts_ref[1:2, :].astype(F32))):
        near, far = values[:, :half], values[:, half:]
        keep_ref[row : row + 1, :] = jnp.where(other, far, near)
        send_ref[row : row + 1, :] = jnp.where(other, near, far)


def add_lanes_kernel(came_count, keep_ref, *refs):
    total = keep_ref[...]
    for ref in refs[:came_count]:
        total += ref[...]
    outs = refs[came_count:]
    lanes = total.shape[1] // len(outs)
    for k, out in enumerate(outs):
        out[...] = total[:, k * lanes : (k + 1) * lanes]


def weight_kernel(tokens, came_count, segments_ref, train_ref, keep_ref, *refs):
    total = keep_ref[...]
    for ref in refs[:came_count]:
        total += ref[...]
    out = refs[came_count]
    own = out.shape[1]
    ref_loss = jnp.log(total[0:1]) - total[1:2]
    places = lax.axis_index(AXIS) * own + lax.broadcasted_iota(I32, (1, own), 1)
    same = (places + 1 < tokens) & (total[2:3].astype(I32) == segments_ref[...])
    out[...] = jnp.where(same, jax.nn.sigmoid(train_ref[...] - ref_loss), 0.0)


def on_device(
    hidden_units, residual, down_weight, final_gain, head_weight, targets, segments, train_loss
):
    own, width = residual.shape
    tokens, depth = hidden_units.shape
    vocab_rows = head_weight.shape[0]
    devices = lax.axis_size(AXIS)
    levels = levels_of(devices, 0)
    gather_levels = [*levels_of(devices, 1)[:-1], levels_of(devices, 0)[-1]]
    sum_levels = levels_of(devices, 1)

    half = (tokens // 2, width)
    gain = final_gain.reshape(-1, 128)
    sources = [hidden_units, targets[None, :], down_weight, residual, gain, segments[None, :], train_loss[None, :]]
    keep, send, facts, residual, gain, segments, train_loss = call(
        functools.partial(ffn_kernel, levels, gather_levels, own, vocab_rows),
        [(half, F32), (half, F32), ((2, tokens), I32)] + [(a.shape, a.dtype) for a in sources[3:]],
        *[pltpu.with_memory_space_constraint(a, pltpu.HBM) for a in sources],
        extra=bytes_of(down_weight),
        scratch=(
            pltpu.VMEM(hidden_units.shape, BF16),
            pltpu.VMEM((1, tokens), I32),
            pltpu.VMEM((CHUNKS, depth, width // CHUNKS), BF16),
            pltpu.SemaphoreType.DMA((CHUNKS,)),
            pltpu.SemaphoreType.DMA((6,)),
        ),
        specs=[IN_HBM] * 7,
    )
    came, rows = [swapped(send.astype(F16), levels[0][1])], tokens // 2
    for level in levels[1:-1]:
        size = len(level)
        rows //= size
        parts = (keep + sum(c.astype(F32) for c in came)).reshape(size, rows, width)
        keep = parts[0]
        came = [swapped(parts[k].astype(F16), level[k]) for k in range(1, size)]
    level = levels[-1]
    size = len(level)
    mine = keep + sum(c.astype(F32) for c in came)
    mine = mine + jnp.pad(residual.astype(F32), ((0, rows - own), (0, 0)))
    blocks = mine.astype(F16).reshape(size, own, width)
    came = [
        swapped(jnp.concatenate([blocks[place ^ k] for place in range(size)]), level[k])
        for k in range(1, size)
    ]
    head_hbm = pltpu.with_memory_space_constraint(head_weight, pltpu.HBM)

    def load(first, count, after):
        return call(
            functools.partial(load_kernel, first),
            [((count, width), BF16)],
            head_hbm,
            after,
            scratch=(pltpu.SemaphoreType.DMA,),
            specs=[IN_HBM, ANYWHERE],
        )[0]

    first = vocab_rows // 2
    heads = [load(0, first, mine)]
    heads[0], *came = lax.optimization_barrier((heads[0], *came))
    total = mine + sum(c.astype(F32) for c in came)
    states, block = call(
        functools.partial(norm_kernel, own),
        [((own, width), BF16), ((rows, width), BF16)],
        total,
        gain,
    )
    heads.append(load(first, vocab_rows - first, states))
    (hidden_states,) = call(copy_kernel, [(states.shape, BF16)], states)
    for level in gather_levels[-2:0:-1]:
        came = [swapped(block, distance) for distance in level[1:]]
        rows *= len(level)
        (block,) = call(
            join_kernel,
            [((rows, width), BF16)],
            heads[-1],
            block,
            *came,
            extra=bytes_of(block) * 8,
            specs=[ANYWHERE] + [WHOLE] * len(level),
        )
    far = swapped(block, gather_levels[0][1])

    keep, send = call(
        functools.partial(loss_kernel, own, gather_levels, sum_levels, len(heads)),
        [((3, tokens // 2), F32)] * 2,
        facts,
        *heads,
        block,
        far,
        extra=2 * bytes_of(block),
    )
    came, lanes = [swapped(send, sum_levels[0][1])], tokens // 2
    for level in sum_levels[1:]:
        lanes //= len(level)
        keep, *parts = call(
            functools.partial(add_lanes_kernel, len(came)), [((3, lanes), F32)] * len(level), keep, *came
        )
        came = [swapped(part, distance) for part, distance in zip(parts, level[1:])]
    (loss_weight,) = call(
        functools.partial(weight_kernel, tokens, len(came)), [((1, own), F32)], segments, train_loss, keep, *came
    )
    return (hidden_states, loss_weight.reshape(own))


def solution(mesh):
    placed = (
        P("groups", "stream"),
        P(("groups", "stream"), None),
        P("stream", None),
        P(),
        P("stream", None),
        P("groups"),
        P(("groups", "stream")),
        P(("groups", "stream")),
    )
    return jax.shard_map(
        on_device,
        mesh=mesh,
        in_specs=placed,
        out_specs=(P(("groups", "stream"), None), P(("groups", "stream"))),
        check_vma=False,
    )
```

```python
import functools

import jax
import jax.numpy as jnp
from jax import lax
from jax.experimental import pallas as pl
from jax.experimental.pallas import tpu as pltpu
from jax.sharding import PartitionSpec as P

AXIS = "stream"
F32 = jnp.float32
BF16 = jnp.bfloat16
F16 = jnp.float16
I32 = jnp.int32
WHOLE = pl.BlockSpec(memory_space=pltpu.VMEM)
IN_HBM = pl.BlockSpec(memory_space=pltpu.HBM)
ANYWHERE = pl.BlockSpec(memory_space=pl.ANY)
CHUNKS = 4


def levels_of(devices, crossed):
    levels, stride = [(0, 1)], 2
    while stride < devices:
        if (devices // stride) % 4 == 0:
            levels.append((0, stride | crossed, 2 * stride | crossed, 3 * stride))
        else:
            levels.append((0, stride | crossed))
        stride *= len(levels[-1])
    assert stride == devices
    return levels


def log2(number):
    assert number & (number - 1) == 0
    return number.bit_length() - 1


def swapped(block, distance):
    return lax.ppermute(block, AXIS, [(i, i ^ distance) for i in range(lax.axis_size(AXIS))])


def bytes_of(*arrays):
    return sum(a.size * a.dtype.itemsize for a in arrays)


def call(body, outs, *operands, extra=0, scratch=(), specs=None):
    shapes = [jax.ShapeDtypeStruct(shape, kind) for shape, kind in outs]
    return pl.pallas_call(
        body,
        out_shape=shapes,
        in_specs=specs or [WHOLE] * len(operands),
        out_specs=[WHOLE] * len(shapes),
        scratch_shapes=scratch,
        compiler_params=pltpu.CompilerParams(
            vmem_limit_bytes=bytes_of(*operands, *shapes) * 5 // 4 + extra + (2 << 20)
        ),
    )(*operands)


def distance_at(holder, levels):
    distance, inner = jnp.zeros_like(holder), 0
    for level in reversed(levels):
        digit = holder >> inner
        for bit in range(log2(len(level))):
            distance ^= ((digit >> bit) & 1) * level[1 << bit]
        inner += log2(len(level))
    return distance


def token_at(place, levels, own):
    distance = distance_at(place >> log2(own), levels)
    return (lax.axis_index(AXIS) ^ distance) * own + (place & (own - 1))


def ffn_kernel(levels, gather_levels, own, vocab_rows, *refs):
    sources, (keep_ref, send_ref, facts_ref, residual_ref, gain_ref, segments_ref, train_ref) = refs[:7], refs[7:14]
    hidden_ref, targets_ref, weights, arrived, loaded = refs[14:]
    hidden_hbm, targets_hbm, down_hbm = sources[:3]
    tokens = hidden_ref.shape[0]
    columns = down_hbm.shape[1] // CHUNKS
    copies = [
        pltpu.make_async_copy(
            down_hbm.at[:, pl.ds(c * columns, columns)], weights.at[c], arrived.at[c]
        )
        for c in range(CHUNKS)
    ]
    pairs = ((hidden_hbm, hidden_ref), (targets_hbm, targets_ref)) + tuple(
        zip(sources[3:], (residual_ref, gain_ref, segments_ref, train_ref))
    )
    small = [pltpu.make_async_copy(*pair, loaded.at[i]) for i, pair in enumerate(pairs)]
    small[0].start()
    for copy in copies + small[1:]:
        copy.start()
    square = (tokens, tokens)
    sublane, lane = (lax.broadcasted_iota(I32, square, d) for d in (0, 1))
    chosen = token_at(sublane, levels, own) == lane
    small[0].wait()
    rows = jnp.dot(
        chosen.astype(F32).astype(BF16), hidden_ref[...], preferred_element_type=F32
    ).astype(BF16)
    for c in range(CHUNKS):
        copies[c].wait()
        part = jnp.dot(rows, weights[c], preferred_element_type=F32)
        keep_ref[:, c * columns : (c + 1) * columns] = part[: tokens // 2]
        send_ref[:, c * columns : (c + 1) * columns] = part[tokens // 2 :]
    for copy in small[1:]:
        copy.wait()
    chosen = token_at(sublane, gather_levels, own) == lane
    wanted = jnp.sum(jnp.where(chosen, targets_ref[...], 0), axis=1, keepdims=True)
    wanted = jnp.sum(jnp.where(sublane == lane, wanted, 0), axis=0, keepdims=True)
    me = lax.axis_index(AXIS)
    facts_ref[0:1, :] = wanted - me * vocab_rows
    at_lane = token_at(lax.broadcasted_iota(I32, (1, tokens), 1), gather_levels, own)
    following = jnp.zeros((1, tokens), I32)
    for j in range(own):
        following = jnp.where(at_lane + 1 == me * own + j, segments_ref[0:1, j : j + 1], following)
    facts_ref[1:2, :] = following


def norm_kernel(own, size, gain_ref, mine_ref, *refs):
    came, (states_ref, normed_ref) = refs[: size - 1], refs[size - 1 :]
    total = mine_ref[...]
    for k in range(1, size):
        order = [place ^ k for place in range(size)]
        total += jnp.concatenate([came[k - 1][p * own : (p + 1) * own, :] for p in order], axis=0)
    states = total.astype(BF16)
    states_ref[...] = states[:own]
    values = states.astype(F32)
    scale = lax.rsqrt(jnp.mean(values * values, axis=1, keepdims=True) + 1e-05)
    for c in range(gain_ref.shape[0]):
        at = slice(c * 128, (c + 1) * 128)
        normed_ref[:, at] = (values[:, at] * scale * gain_ref[c : c + 1, :].astype(F32)).astype(BF16)


def copy_kernel(source, after, out):
    out[...] = source[...]


def load_kernel(first, source, after, out, arrived):
    copy = pltpu.make_async_copy(source.at[pl.ds(first, out.shape[0])], out, arrived)
    copy.start()
    copy.wait()


def join_kernel(*refs):
    blocks, out = refs[1:-1], refs[-1]
    out[...] = jnp.concatenate([b[...].astype(F32) for b in blocks], axis=0).astype(BF16)


def loss_kernel(own, gather_levels, sum_levels, head_count, facts_ref, *refs):
    heads, (near_ref, far_ref, keep_ref, send_ref) = refs[:head_count], refs[head_count:]
    rows = jnp.concatenate([near_ref[...], far_ref[...]], axis=0)
    half, first, total, picked = rows.shape[0] // 2, 0, 0.0, 0.0
    for head_ref in heads:
        logits = lax.dot_general(
            head_ref[...], rows, (((1,), (1,)), ((), ())), preferred_element_type=F32
        )
        ids = lax.broadcasted_iota(I32, logits.shape, 0) + first
        total += jnp.sum(jnp.exp(logits), axis=0, keepdims=True)
        picked += jnp.sum(jnp.where(ids == facts_ref[0:1, :], logits, 0.0), axis=0, keepdims=True)
        first += head_ref.shape[0]
    holder = lax.broadcasted_iota(I32, (1, half), 1) >> log2(own)
    other = ((distance_at(holder, gather_levels[1:]) ^ distance_at(holder, sum_levels[1:])) & 1) == 1
    for row, values in enumerate((total, picked, facts_ref[1:2, :].astype(F32))):
        near, far = values[:, :half], values[:, half:]
        keep_ref[row : row + 1, :] = jnp.where(other, far, near)
        send_ref[row : row + 1, :] = jnp.where(other, near, far)


def add_lanes_kernel(came_count, keep_ref, *refs):
    total = keep_ref[...]
    for ref in refs[:came_count]:
        total += ref[...]
    outs = refs[came_count:]
    lanes = total.shape[1] // len(outs)
    for k, out in enumerate(outs):
        out[...] = total[:, k * lanes : (k + 1) * lanes]


def weight_kernel(tokens, came_count, segments_ref, train_ref, keep_ref, *refs):
    total = keep_ref[...]
    for ref in refs[:came_count]:
        total += ref[...]
    out = refs[came_count]
    own = out.shape[1]
    ref_loss = jnp.log(total[0:1]) - total[1:2]
    places = lax.axis_index(AXIS) * own + lax.broadcasted_iota(I32, (1, own), 1)
    same = (places + 1 < tokens) & (total[2:3].astype(I32) == segments_ref[...])
    out[...] = jnp.where(same, jax.nn.sigmoid(train_ref[...] - ref_loss), 0.0)


def on_device(
    hidden_units, residual, down_weight, final_gain, head_weight, targets, segments, train_loss
):
    own, width = residual.shape
    tokens, depth = hidden_units.shape
    vocab_rows = head_weight.shape[0]
    devices = lax.axis_size(AXIS)
    levels = levels_of(devices, 0)
    gather_levels = [*levels_of(devices, 1)[:-1], levels_of(devices, 0)[-1]]
    sum_levels = levels_of(devices, 1)

    half = (tokens // 2, width)
    gain = final_gain.reshape(-1, 128)
    sources = [hidden_units, targets[None, :], down_weight, residual, gain, segments[None, :], train_loss[None, :]]
    keep, send, facts, residual, gain, segments, train_loss = call(
        functools.partial(ffn_kernel, levels, gather_levels, own, vocab_rows),
        [(half, F32), (half, F32), ((2, tokens), I32)] + [(a.shape, a.dtype) for a in sources[3:]],
        *[pltpu.with_memory_space_constraint(a, pltpu.HBM) for a in sources],
        extra=bytes_of(down_weight),
        scratch=(
            pltpu.VMEM(hidden_units.shape, BF16),
            pltpu.VMEM((1, tokens), I32),
            pltpu.VMEM((CHUNKS, depth, width // CHUNKS), BF16),
            pltpu.SemaphoreType.DMA((CHUNKS,)),
            pltpu.SemaphoreType.DMA((6,)),
        ),
        specs=[IN_HBM] * 7,
    )
    came, rows = [swapped(send.astype(F16), levels[0][1])], tokens // 2
    for level in levels[1:-1]:
        size = len(level)
        rows //= size
        parts = (keep + sum(c.astype(F32) for c in came)).reshape(size, rows, width)
        keep = parts[0]
        came = [swapped(parts[k].astype(F16), level[k]) for k in range(size - 1, 0, -1)]
    level = levels[-1]
    size = len(level)
    mine = keep + sum(c.astype(F32) for c in came)
    mine = mine + jnp.pad(residual.astype(F32), ((0, rows - own), (0, 0)))
    came = [swapped(mine.astype(F16), level[k]) for k in range(1, size)]
    head_hbm = pltpu.with_memory_space_constraint(head_weight, pltpu.HBM)

    def load(first, count, after):
        return call(
            functools.partial(load_kernel, first),
            [((count, width), BF16)],
            head_hbm,
            after,
            scratch=(pltpu.SemaphoreType.DMA,),
            specs=[IN_HBM, ANYWHERE],
        )[0]

    first = vocab_rows // 2
    heads = [load(0, first, mine)]
    heads[0], *came = lax.optimization_barrier((heads[0], *came))
    states, block = call(
        functools.partial(norm_kernel, own, size),
        [((own, width), BF16), ((rows, width), BF16)],
        gain,
        mine,
        *[c.astype(F32) for c in came],
    )
    heads.append(load(first, vocab_rows - first, states))
    for level in gather_levels[-2:0:-1]:
        came = [swapped(block, distance) for distance in level[1:]]
        rows *= len(level)
        (block,) = call(
            join_kernel,
            [((rows, width), BF16)],
            heads[-1],
            block,
            *came,
            extra=bytes_of(block) * 8,
            specs=[ANYWHERE] + [WHOLE] * len(level),
        )
    far = swapped(block, gather_levels[0][1])

    keep, send = call(
        functools.partial(loss_kernel, own, gather_levels, sum_levels, len(heads)),
        [((3, tokens // 2), F32)] * 2,
        facts,
        *heads,
        block,
        far,
        extra=2 * bytes_of(block),
    )
    came, lanes = [swapped(send, sum_levels[0][1])], tokens // 2
    for level in sum_levels[1:]:
        lanes //= len(level)
        keep, *parts = call(
            functools.partial(add_lanes_kernel, len(came)), [((3, lanes), F32)] * len(level), keep, *came
        )
        sends = list(zip(parts, level[1:]))
        came = [swapped(*send) for send in sends[-1:] + sends[:-1]]
        if level is sum_levels[1]:
            (hidden_states,) = call(
                copy_kernel, [(states.shape, BF16)], states, came[0], specs=[WHOLE, ANYWHERE]
            )
    (loss_weight,) = call(
        functools.partial(weight_kernel, tokens, len(came)), [((1, own), F32)], segments, train_loss, keep, *came
    )
    return (hidden_states, loss_weight.reshape(own))


def solution(mesh):
    placed = (
        P("groups", "stream"),
        P(("groups", "stream"), None),
        P("stream", None),
        P(),
        P("stream", None),
        P("groups"),
        P(("groups", "stream")),
        P(("groups", "stream")),
    )
    return jax.shard_map(
        on_device,
        mesh=mesh,
        in_specs=placed,
        out_specs=(P(("groups", "stream"), None), P(("groups", "stream"))),
        check_vma=False,
    )
```

```python
import functools

import jax
import jax.numpy as jnp
from jax import lax
from jax.experimental import pallas as pl
from jax.experimental.pallas import tpu as pltpu
from jax.sharding import PartitionSpec as P

AXIS = "stream"
F32 = jnp.float32
BF16 = jnp.bfloat16
F16 = jnp.float16
I32 = jnp.int32
WHOLE = pl.BlockSpec(memory_space=pltpu.VMEM)
IN_HBM = pl.BlockSpec(memory_space=pltpu.HBM)
ANYWHERE = pl.BlockSpec(memory_space=pl.ANY)
CHUNKS = 4


def levels_of(devices, quad=(0, 0, 0), pair=0):
    levels, stride = [(0, 1)], 2
    while stride < devices:
        if (devices // stride) % 4 == 0:
            levels.append((0, *(k * stride | quad[k - 1] for k in (1, 2, 3))))
        else:
            levels.append((0, stride | pair))
        stride *= len(levels[-1])
    assert stride == devices
    return levels


def log2(number):
    assert number & (number - 1) == 0
    return number.bit_length() - 1


def swapped(block, distance):
    return lax.ppermute(block, AXIS, [(i, i ^ distance) for i in range(lax.axis_size(AXIS))])


def bytes_of(*arrays):
    return sum(a.size * a.dtype.itemsize for a in arrays)


def call(body, outs, *operands, extra=0, scratch=(), specs=None):
    shapes = [jax.ShapeDtypeStruct(shape, kind) for shape, kind in outs]
    return pl.pallas_call(
        body,
        out_shape=shapes,
        in_specs=specs or [WHOLE] * len(operands),
        out_specs=[WHOLE] * len(shapes),
        scratch_shapes=scratch,
        compiler_params=pltpu.CompilerParams(
            vmem_limit_bytes=bytes_of(*operands, *shapes) * 5 // 4 + extra + (2 << 20)
        ),
    )(*operands)


def distance_at(holder, levels):
    distance, inner = jnp.zeros_like(holder), 0
    for level in reversed(levels):
        digit = holder >> inner
        for bit in range(log2(len(level))):
            distance ^= ((digit >> bit) & 1) * level[1 << bit]
        inner += log2(len(level))
    return distance


def token_at(place, levels, own):
    distance = distance_at(place >> log2(own), levels)
    return (lax.axis_index(AXIS) ^ distance) * own + (place & (own - 1))


def ffn_kernel(levels, gather_levels, own, vocab_rows, *refs):
    sources, (keep_ref, send_ref, facts_ref, residual_ref, gain_ref, segments_ref, train_ref) = refs[:7], refs[7:14]
    hidden_ref, targets_ref, weights, arrived, loaded = refs[14:]
    hidden_hbm, targets_hbm, down_hbm = sources[:3]
    tokens = hidden_ref.shape[0]
    columns = down_hbm.shape[1] // CHUNKS
    copies = [
        pltpu.make_async_copy(
            down_hbm.at[:, pl.ds(c * columns, columns)], weights.at[c], arrived.at[c]
        )
        for c in range(CHUNKS)
    ]
    pairs = ((hidden_hbm, hidden_ref), (targets_hbm, targets_ref)) + tuple(
        zip(sources[3:], (residual_ref, gain_ref, segments_ref, train_ref))
    )
    small = [pltpu.make_async_copy(*pair, loaded.at[i]) for i, pair in enumerate(pairs)]
    small[0].start()
    for copy in copies + small[1:]:
        copy.start()
    square = (tokens, tokens)
    sublane, lane = (lax.broadcasted_iota(I32, square, d) for d in (0, 1))
    chosen = token_at(sublane, levels, own) == lane
    small[0].wait()
    rows = jnp.dot(
        chosen.astype(F32).astype(BF16), hidden_ref[...], preferred_element_type=F32
    ).astype(BF16)
    for c in range(CHUNKS):
        copies[c].wait()
        part = jnp.dot(rows, weights[c], preferred_element_type=F32)
        keep_ref[:, c * columns : (c + 1) * columns] = part[: tokens // 2]
        send_ref[:, c * columns : (c + 1) * columns] = part[tokens // 2 :]
    for copy in small[1:]:
        copy.wait()
    chosen = token_at(sublane, gather_levels, own) == lane
    wanted = jnp.sum(jnp.where(chosen, targets_ref[...], 0), axis=1, keepdims=True)
    wanted = jnp.sum(jnp.where(sublane == lane, wanted, 0), axis=0, keepdims=True)
    me = lax.axis_index(AXIS)
    facts_ref[0:1, :] = wanted - me * vocab_rows
    at_lane = token_at(lax.broadcasted_iota(I32, (1, tokens), 1), gather_levels, own)
    following = jnp.zeros((1, tokens), I32)
    for j in range(own):
        following = jnp.where(at_lane + 1 == me * own + j, segments_ref[0:1, j : j + 1], following)
    facts_ref[1:2, :] = following


def norm_kernel(own, size, gain_ref, mine_ref, *refs):
    came, (states_ref, normed_ref) = refs[: size - 1], refs[size - 1 :]
    total = mine_ref[...]
    for k in range(1, size):
        order = [place ^ k for place in range(size)]
        total += jnp.concatenate([came[k - 1][p * own : (p + 1) * own, :] for p in order], axis=0)
    states = total.astype(BF16)
    states_ref[...] = states[:own]
    values = states.astype(F32)
    scale = lax.rsqrt(jnp.mean(values * values, axis=1, keepdims=True) + 1e-05)
    for c in range(gain_ref.shape[0]):
        at = slice(c * 128, (c + 1) * 128)
        normed_ref[:, at] = (values[:, at] * scale * gain_ref[c : c + 1, :].astype(F32)).astype(BF16)


def copy_kernel(source, after, out):
    out[...] = source[...]


def load_kernel(first, source, after, out, arrived):
    copy = pltpu.make_async_copy(source.at[pl.ds(first, out.shape[0])], out, arrived)
    copy.start()
    copy.wait()


def join_kernel(*refs):
    blocks, out = refs[1:-1], refs[-1]
    out[...] = jnp.concatenate([b[...].astype(F32) for b in blocks], axis=0).astype(BF16)


def loss_kernel(own, gather_levels, sum_levels, head_count, facts_ref, *refs):
    heads, (near_ref, far_ref, keep_ref, send_ref) = refs[:head_count], refs[head_count:]
    rows = jnp.concatenate([near_ref[...], far_ref[...]], axis=0)
    half, first, total, picked = rows.shape[0] // 2, 0, 0.0, 0.0
    for head_ref in heads:
        logits = lax.dot_general(
            head_ref[...], rows, (((1,), (1,)), ((), ())), preferred_element_type=F32
        )
        ids = lax.broadcasted_iota(I32, logits.shape, 0) + first
        total += jnp.sum(jnp.exp(logits), axis=0, keepdims=True)
        picked += jnp.sum(jnp.where(ids == facts_ref[0:1, :], logits, 0.0), axis=0, keepdims=True)
        first += head_ref.shape[0]
    holder = lax.broadcasted_iota(I32, (1, half), 1) >> log2(own)
    other = ((distance_at(holder, gather_levels[1:]) ^ distance_at(holder, sum_levels[1:])) & 1) == 1
    for row, values in enumerate((total, picked, facts_ref[1:2, :].astype(F32))):
        near, far = values[:, :half], values[:, half:]
        keep_ref[row : row + 1, :] = jnp.where(other, far, near)
        send_ref[row : row + 1, :] = jnp.where(other, near, far)


def add_lanes_kernel(came_count, keep_ref, *refs):
    total = keep_ref[...]
    for ref in refs[:came_count]:
        total += ref[...]
    outs = refs[came_count:]
    lanes = total.shape[1] // len(outs)
    for k, out in enumerate(outs):
        out[...] = total[:, k * lanes : (k + 1) * lanes]


def weight_kernel(tokens, came_count, segments_ref, train_ref, keep_ref, *refs):
    total = keep_ref[...]
    for ref in refs[:came_count]:
        total += ref[...]
    out = refs[came_count]
    own = out.shape[1]
    ref_loss = jnp.log(total[0:1]) - total[1:2]
    places = lax.axis_index(AXIS) * own + lax.broadcasted_iota(I32, (1, own), 1)
    same = (places + 1 < tokens) & (total[2:3].astype(I32) == segments_ref[...])
    out[...] = jnp.where(same, jax.nn.sigmoid(train_ref[...] - ref_loss), 0.0)


def on_device(
    hidden_units, residual, down_weight, final_gain, head_weight, targets, segments, train_loss
):
    own, width = residual.shape
    tokens, depth = hidden_units.shape
    vocab_rows = head_weight.shape[0]
    devices = lax.axis_size(AXIS)
    levels = levels_of(devices)
    gather_levels = [*levels_of(devices, (1, 0, 1))[:-1], levels[-1]]
    sum_levels = levels_of(devices, (1, 1, 0), 1)

    half = (tokens // 2, width)
    gain = final_gain.reshape(-1, 128)
    sources = [hidden_units, targets[None, :], down_weight, residual, gain, segments[None, :], train_loss[None, :]]
    keep, send, facts, residual, gain, segments, train_loss = call(
        functools.partial(ffn_kernel, levels, gather_levels, own, vocab_rows),
        [(half, F32), (half, F32), ((2, tokens), I32)] + [(a.shape, a.dtype) for a in sources[3:]],
        *[pltpu.with_memory_space_constraint(a, pltpu.HBM) for a in sources],
        extra=bytes_of(down_weight),
        scratch=(
            pltpu.VMEM(hidden_units.shape, BF16),
            pltpu.VMEM((1, tokens), I32),
            pltpu.VMEM((CHUNKS, depth, width // CHUNKS), BF16),
            pltpu.SemaphoreType.DMA((CHUNKS,)),
            pltpu.SemaphoreType.DMA((6,)),
        ),
        specs=[IN_HBM] * 7,
    )
    came, rows = [swapped(send.astype(F16), levels[0][1])], tokens // 2
    for level in levels[1:-1]:
        size = len(level)
        rows //= size
        parts = (keep + sum(c.astype(F32) for c in came)).reshape(size, rows, width)
        keep = parts[0]
        came = [swapped(parts[k].astype(F16), level[k]) for k in range(size - 1, 0, -1)]
    level = levels[-1]
    size = len(level)
    mine = keep + sum(c.astype(F32) for c in came)
    mine = mine + jnp.pad(residual.astype(F32), ((0, rows - own), (0, 0)))
    came = [swapped(mine.astype(F16), level[k]) for k in range(1, size)]
    head_hbm = pltpu.with_memory_space_constraint(head_weight, pltpu.HBM)

    def load(first, count, after):
        return call(
            functools.partial(load_kernel, first),
            [((count, width), BF16)],
            head_hbm,
            after,
            scratch=(pltpu.SemaphoreType.DMA,),
            specs=[IN_HBM, ANYWHERE],
        )[0]

    first = vocab_rows // 2
    heads = [load(0, first, mine)]
    heads[0], *came = lax.optimization_barrier((heads[0], *came))
    states, block = call(
        functools.partial(norm_kernel, own, size),
        [((own, width), BF16), ((rows, width), BF16)],
        gain,
        mine,
        *[c.astype(F32) for c in came],
    )
    heads.append(load(first, vocab_rows - first, states))
    for level in gather_levels[-2:0:-1]:
        came = [swapped(block, distance) for distance in level[1:]]
        rows *= len(level)
        (block,) = call(
            join_kernel,
            [((rows, width), BF16)],
            heads[-1],
            block,
            *came,
            extra=bytes_of(block) * 8,
            specs=[ANYWHERE] + [WHOLE] * len(level),
        )
    far = swapped(block, gather_levels[0][1])

    keep, send = call(
        functools.partial(loss_kernel, own, gather_levels, sum_levels, len(heads)),
        [((3, tokens // 2), F32)] * 2,
        facts,
        *heads,
        block,
        far,
        extra=2 * bytes_of(block),
    )
    came, lanes = [swapped(send, sum_levels[0][1])], tokens // 2
    for level in sum_levels[1:]:
        lanes //= len(level)
        keep, *parts = call(
            functools.partial(add_lanes_kernel, len(came)), [((3, lanes), F32)] * len(level), keep, *came
        )
        sends = list(zip(parts, level[1:]))
        came = [swapped(*send) for send in sends[-1:] + sends[:-1]]
        if level is sum_levels[1]:
            (hidden_states,) = call(
                copy_kernel, [(states.shape, BF16)], states, came[0], specs=[WHOLE, ANYWHERE]
            )
    (loss_weight,) = call(
        functools.partial(weight_kernel, tokens, len(came)), [((1, own), F32)], segments, train_loss, keep, *came
    )
    return (hidden_states, loss_weight.reshape(own))


def solution(mesh):
    placed = (
        P("groups", "stream"),
        P(("groups", "stream"), None),
        P("stream", None),
        P(),
        P("stream", None),
        P("groups"),
        P(("groups", "stream")),
        P(("groups", "stream")),
    )
    return jax.shard_map(
        on_device,
        mesh=mesh,
        in_specs=placed,
        out_specs=(P(("groups", "stream"), None), P(("groups", "stream"))),
        check_vma=False,
    )
```
